32 devices in a mesh: scene: 4 (over x, core), tile: 8 (over z, y).
Axes of the slice: x: 2, y: 2, z: 4, core: 2. Of those that a mesh axis runs over, the one named last changes fastest.
Arguments:
- image: bfloat16 [4, 8, 24, 32, 768], P('scene', 'tile'), may hold values from -6 to 6
- kernel: float32 [7, 7, 768], replicated, may hold values from -0.875 to 0.875
- ln_gain: float32 [768], replicated, may hold values from 0.5 to 2
- w_in: bfloat16 [768, 3072], replicated, may hold values from -0.21875 to 0.21875
- bias_in: float32 [3072], replicated, may hold values from -3 to 3
- w_out: bfloat16 [3072, 768], replicated, may hold values from -0.109375 to 0.109375
- layer_scale: float32 [768], replicated, may hold values from 0.5 to 2
- grad_rows: bfloat16 [26624, 768], P(('scene', 'tile')), may hold values from -6 to 6
- return_pos: int32 [26624], P(('scene', 'tile')), may hold values from 0 to 24575, as said below
- send_counts: int32 [32, 32], P(('scene', 'tile')), may hold values from 0 to 48, as said below
- send_offsets: int32 [32, 32], P(('scene', 'tile')), may hold values from 0 to 832, as said below
Outputs:
- grad_input: bfloat16 [4, 8, 24, 32, 768], P('scene', 'tile')
- grad_w_in: float32 [768, 3072], P(('scene', 'tile'))
- grad_w_out: float32 [3072, 768], P(('scene', 'tile'))
- grad_kernel: float32 [7, 7, 768], replicated
The draws below stay inside these ranges and needn't reach their ends.
Inputs may be any that keep to these rules, and one draw needn't show every extreme that they name: `return_pos`: every row, live or not, lies in the segment d of its owner with the largest send_offsets[o, d] <= r, and names a position of device d's tile (between d * 768 and (d + 1) * 768 - 1); positions may repeat. `send_counts`: each owner has 768 live rows in all, at most 48 for one device, and exactly 48 for at least one device. For each owner, send_offsets[o, 0] = 0 and send_offsets[o, d + 1] - send_offsets[o, d] - send_counts[o, d] is 0, 1 or 2.
All inputs are finite; a program needn't handle non-finite values.
Results may differ from the reference program's by a relative error of at most 0.0064.
Values may be sent and summed in bfloat16 or wider, within the bound.
A program may use at most 128 MiB of HBM per device.

```python
import math
import jax
import jax.numpy as jnp
from jax import lax

C = 768
HID = 3072
KS = 7
TH = 24
TW = 32
GRID_W = 4
PEERS = 32
ROWS = 768
CAP = 48
OWN_ROWS = 832
POSITIONS = 24576
N_SCENE = 4
N_TILE = 8


def return_lists(key):
    base_key = jax.random.fold_in(key, 4242)
    key_hot, key_owner = jax.random.split(base_key)
    hotness = jax.random.randint(key_hot, (PEERS,), 0, 4)
    slot_owner = jnp.arange(PEERS * CAP, dtype=jnp.int32) // CAP

    def one_owner(owner_key):
        key_score, key_favour, key_gap, key_place = jax.random.split(owner_key, 4)
        noise_score = jax.random.randint(key_score, (PEERS * CAP,), 0, 1024)
        favourite = jax.random.randint(key_favour, (), 0, PEERS)
        score_total = noise_score + hotness[slot_owner] * 256 + (slot_owner == favourite).astype(jnp.int32) * 8192
        distinct = score_total * (PEERS * CAP) + jnp.arange(PEERS * CAP, dtype=jnp.int32)
        _, chosen = lax.top_k(distinct, ROWS)
        picked = jnp.zeros((PEERS * CAP,), jnp.int32).at[chosen].set(1)
        counts = jnp.sum(picked.reshape(PEERS, CAP), axis=1).astype(jnp.int32)
        gap_rows = jax.random.randint(key_gap, (PEERS,), 0, 3)
        seg_length = counts + gap_rows
        offsets = (jnp.cumsum(seg_length) - seg_length).astype(jnp.int32)
        row_index = jnp.arange(OWN_ROWS, dtype=jnp.int32)
        segment = jnp.sum((offsets[None, :] <= row_index[:, None]).astype(jnp.int32), axis=1).astype(jnp.int32) - 1
        local_pixel = jax.random.randint(key_place, (OWN_ROWS,), 0, ROWS)
        positions = segment * ROWS + local_pixel
        return (counts, offsets, positions)
    counts, offsets, positions = jax.vmap(one_owner)(jax.random.split(key_owner, PEERS))
    return (counts, offsets, positions.reshape(-1))


def draw_return_pos(key, part):
    return return_lists(key)[2]


def draw_send_counts(key, part):
    return return_lists(key)[0]


def draw_send_offsets(key, part):
    return return_lists(key)[1]


def block_scale(own_key, shape, pieces, least, high):
    def one(dim, blocks):
        steps = jax.random.uniform(jax.random.fold_in(jax.random.fold_in(own_key, 6), dim), (blocks,), jnp.float32, least / len(pieces), high / len(pieces))
        return jnp.repeat(jnp.exp(steps), shape[dim] // blocks).reshape((-1,) + (1,) * (len(shape) - dim - 1))

    loudness = one(*pieces[0])
    for cut in pieces[1:]:
        loudness = loudness * one(*cut)
    return loudness


def noise(key, shape, scale, reach, pieces=(), kind=jnp.bfloat16):
    array = scale * jax.random.normal(key, shape, jnp.float32)
    if pieces:
        array = array * block_scale(key, shape, pieces, -0.22, 0.18)
    return jnp.clip(array, -reach, reach).astype(kind)


def setup_inputs(seed: int = 0) -> dict:
    seeds = jax.random.split(jax.random.key(seed), 12)
    image = noise(seeds[0], (N_SCENE, N_TILE, TH, TW, C), 1.0, 6.0, ((0, 4), (1, 8)))
    kernel = noise(seeds[1], (KS, KS, C), (KS * KS) ** -0.5, 0.875, (), jnp.float32)
    ln_gain = jnp.clip(jnp.exp(jax.random.uniform(seeds[2], (C,), jnp.float32, math.log(0.5), math.log(2.0))), 0.5, 2.0)
    w_in = noise(seeds[3], (C, HID), C ** -0.5, 0.21875)
    bias_in = noise(seeds[4], (HID,), 0.7, 3.0, (), jnp.float32)
    w_out = noise(seeds[5], (HID, C), HID ** -0.5, 0.109375)
    layer_scale = jnp.clip(jnp.exp(jax.random.uniform(seeds[6], (C,), jnp.float32, math.log(0.5), math.log(2.0))), 0.5, 2.0)
    grad_rows = noise(seeds[7], (PEERS * OWN_ROWS, C), 1.0, 6.0, ((0, 32),))
    return_pos = draw_return_pos(jax.random.fold_in(seeds[11], 71), 0)
    send_counts = draw_send_counts(jax.random.fold_in(seeds[11], 71), 0)
    send_offsets = draw_send_offsets(jax.random.fold_in(seeds[11], 71), 0)
    return dict(image=image, kernel=kernel, ln_gain=ln_gain, w_in=w_in, bias_in=bias_in, w_out=w_out, layer_scale=layer_scale, grad_rows=grad_rows, return_pos=return_pos, send_counts=send_counts, send_offsets=send_offsets)


EPSILON = 1e-06
SQRT_TWO_PI = 0.7978845608028654
CUBIC = 0.044715

def depthwise(padded, kernel, height, breadth):
    result = jnp.zeros((height, breadth, padded.shape[2]), jnp.float32)
    for k_row in range(KS):
        for k_col in range(KS):
            result = result + kernel[k_row, k_col] * padded[k_row:k_row + height, k_col:k_col + breadth]
    return result

def kernel_terms(upstream, padded, height, breadth):
    return jnp.stack([jnp.stack([lax.optimization_barrier(jnp.sum(upstream * padded[k_row:k_row + height, k_col:k_col + breadth], axis=(0, 1))) for k_col in range(KS)]) for k_row in range(KS)])

def gelu_pair(hidden):
    inner_arg = SQRT_TWO_PI * (hidden + CUBIC * hidden * hidden * hidden)
    tangent = jnp.tanh(inner_arg)
    activated = 0.5 * hidden * (1.0 + tangent)
    derivative = 0.5 * (1.0 + tangent) + 0.5 * hidden * (1.0 - tangent * tangent) * SQRT_TWO_PI * (1.0 + 3.0 * CUBIC * hidden * hidden)
    return (activated, derivative)

def to_image(scene_tiles):
    grid_rows = N_TILE // GRID_W
    return scene_tiles.reshape(grid_rows, GRID_W, TH, TW, -1).transpose(0, 2, 1, 3, 4).reshape(grid_rows * TH, GRID_W * TW, -1)

def from_image(picture):
    grid_rows = N_TILE // GRID_W
    return picture.reshape(grid_rows, TH, GRID_W, TW, -1).transpose(0, 2, 1, 3, 4).reshape(N_TILE, TH, TW, -1)

def live_rows(counts, offsets):
    row_index = jnp.arange(OWN_ROWS, dtype=jnp.int32)
    segment = lax.optimization_barrier(jnp.sum((offsets[None, :] <= row_index[:, None]).astype(jnp.int32), axis=1)).astype(jnp.int32) - 1
    segment = jnp.clip(segment, 0, PEERS - 1)
    segment_end = offsets[segment] + counts[segment]
    return row_index < segment_end

def reference(image, kernel, ln_gain, w_in, bias_in, w_out, layer_scale, grad_rows, return_pos, send_counts, send_offsets):
    alive = jax.vmap(live_rows)(send_counts, send_offsets).reshape(-1)
    live_terms = jnp.where(alive[:, None], grad_rows.astype(jnp.float32), jnp.float32(0.0))
    cotangent = jnp.zeros((POSITIONS, C), jnp.float32).at[return_pos].add(live_terms)
    cotangent = cotangent.reshape(N_SCENE, N_TILE, TH, TW, C)
    height = N_TILE // GRID_W * TH
    breadth = GRID_W * TW
    halo_width = KS // 2
    flipped = kernel[::-1, ::-1]
    spread = ((halo_width, halo_width), (halo_width, halo_width), (0, 0))

    def per_scene(running, inputs):
        sum_in, sum_out, sum_kernel = running
        scene_tiles, upstream_tiles = inputs
        picture = to_image(scene_tiles).astype(jnp.float32)
        padded = jnp.pad(picture, spread)
        mixed_sum = depthwise(padded, kernel, height, breadth).reshape(-1, C)
        centre = mixed_sum - lax.optimization_barrier(jnp.mean(mixed_sum, axis=-1, keepdims=True))
        inv_std = lax.rsqrt(lax.optimization_barrier(jnp.mean(centre * centre, axis=-1, keepdims=True)) + EPSILON)
        normed = centre * inv_std
        scaled = (normed * ln_gain).astype(jnp.bfloat16)
        hidden = jnp.dot(scaled, w_in, preferred_element_type=jnp.float32) + bias_in
        activated, derivative = gelu_pair(hidden)
        act_low = activated.astype(jnp.bfloat16)
        upstream = to_image(upstream_tiles).reshape(-1, C)
        branch_grad = (upstream * layer_scale).astype(jnp.bfloat16)
        sum_out = sum_out + jnp.dot(act_low.T, branch_grad, preferred_element_type=jnp.float32)
        act_grad = jnp.dot(branch_grad, w_out.T, preferred_element_type=jnp.float32)
        hidden_grad = (act_grad * derivative).astype(jnp.bfloat16)
        sum_in = sum_in + jnp.dot(scaled.T, hidden_grad, preferred_element_type=jnp.float32)
        normed_grad = jnp.dot(hidden_grad, w_in.T, preferred_element_type=jnp.float32) * ln_gain
        mixed_grad = inv_std * (normed_grad - lax.optimization_barrier(jnp.mean(normed_grad, axis=-1, keepdims=True)) - normed * lax.optimization_barrier(jnp.mean(normed_grad * normed, axis=-1, keepdims=True)))
        mixed_low = lax.optimization_barrier(mixed_grad.astype(jnp.bfloat16)).astype(jnp.float32)
        grad_picture = mixed_low.reshape(height, breadth, C)
        sum_kernel = sum_kernel + kernel_terms(grad_picture, padded, height, breadth)
        through = depthwise(jnp.pad(grad_picture, spread), flipped, height, breadth)
        grad_tiles = from_image((upstream.reshape(height, breadth, C) + through).astype(jnp.bfloat16))
        return ((sum_in, sum_out, sum_kernel), grad_tiles)
    initial = (jnp.zeros((C, HID), jnp.float32), jnp.zeros((HID, C), jnp.float32), jnp.zeros((KS, KS, C), jnp.float32))
    (sum_in, sum_out, sum_kernel), grad_input = lax.scan(per_scene, initial, (image, cotangent))
    factor = jnp.float32(1.0 / math.sqrt(POSITIONS))
    kernel_factor = jnp.float32(1.0 / math.sqrt(GRID_W * GRID_W * ROWS))
    return (grad_input, sum_in * factor, sum_out * factor, sum_kernel * kernel_factor)
```

```python
import math

import jax
import jax.numpy as jnp
from jax import lax
from jax.experimental import pallas as pl
from jax.experimental.pallas import tpu as pltpu
from jax.sharding import PartitionSpec as P

KS = 7
GRID_W = 4


EPSILON = 1e-06
SQRT_TWO_PI = 0.7978845608028654
CUBIC = 0.044715


LANES = 128
GROUP = 4


def widen(padded_ref, wide_ref):
    rows, cols = padded_ref.shape[0], padded_ref.shape[1]

    @pl.loop(0, rows)
    def _(row):
        wide_ref[row, pl.ds(0, cols), :] = padded_ref[row].astype(jnp.float32)


def conv_rows(wide_ref, kernel_ref, first, breadth, flip):
    sums = [jnp.zeros((breadth, LANES), jnp.float32) for _ in range(GROUP)]
    for col in range(KS):
        for row in range(GROUP + KS - 1):
            piece = wide_ref[first + row, pl.ds(col, breadth), :]
            for out in range(GROUP):
                tap = row - out
                if 0 <= tap < KS:
                    k_row, k_col = (KS - 1 - tap, KS - 1 - col) if flip else (tap, col)
                    sums[out] = sums[out] + kernel_ref[k_row, pl.ds(k_col, 1), :] * piece
    return sums


def forward_body(padded_ref, kernel_ref, out_ref, wide_ref):
    height, breadth = out_ref.shape[0], out_ref.shape[1]
    widen(padded_ref, wide_ref)

    @pl.loop(0, height // GROUP)
    def _(group):
        first = group * GROUP
        sums = conv_rows(wide_ref, kernel_ref, first, breadth, False)
        for out in range(GROUP):
            out_ref[first + out] = sums[out]


def backward_body(padded_ref, kernel_ref, up_ref, out_ref, wide_ref):
    height, breadth = out_ref.shape[0], out_ref.shape[1]
    widen(padded_ref, wide_ref)

    @pl.loop(0, height // GROUP)
    def _(group):
        first = group * GROUP
        sums = conv_rows(wide_ref, kernel_ref, first, breadth, True)
        for out in range(GROUP):
            out_ref[first + out] = (sums[out] + up_ref[first + out]).astype(out_ref.dtype)


def terms_body(grad_ref, padded_ref, out_ref, wide_ref):
    height, breadth = grad_ref.shape[0], grad_ref.shape[1]
    widen(padded_ref, wide_ref)
    for col in range(KS):

        def step(group, sums):
            first = group * GROUP
            sums = list(sums)
            grads = [grad_ref[first + out].astype(jnp.float32) for out in range(GROUP)]
            for row in range(GROUP + KS - 1):
                piece = wide_ref[first + row, pl.ds(col, breadth), :]
                for out in range(GROUP):
                    tap = row - out
                    if 0 <= tap < KS:
                        prod = (grads[out] * piece).reshape(breadth // 8, 8, LANES)
                        sums[tap] = sums[tap] + jnp.sum(prod, axis=0)
            return tuple(sums)

        zeros = tuple(jnp.zeros((8, LANES), jnp.float32) for _ in range(KS))
        sums = lax.fori_loop(0, height // GROUP, step, zeros)
        for tap in range(KS):
            out_ref[tap, pl.ds(col, 1), :] = jnp.sum(sums[tap], axis=0, keepdims=True)


def by_lanes(shape):
    return pl.BlockSpec(tuple(shape[:2]) + (LANES,), lambda lane: (0, 0, lane))


def lane_call(body, args, out_shape, out_type, wide):
    flops = 2 * KS * KS * wide[0] * wide[1] * out_shape[2]
    return pl.pallas_call(
        body,
        out_shape=jax.ShapeDtypeStruct(out_shape, out_type),
        grid=(out_shape[2] // LANES,),
        in_specs=[by_lanes(arg.shape) for arg in args],
        out_specs=by_lanes(out_shape),
        scratch_shapes=[pltpu.VMEM((wide[0], -(-wide[1] // 8) * 8, LANES), jnp.float32)],
        compiler_params=pltpu.CompilerParams(vmem_limit_bytes=24 * 2**20),
        cost_estimate=pl.CostEstimate(flops=flops * 100, bytes_accessed=40 * 2**20, transcendentals=0),
    )(*args)


def extend(block):
    halo = KS // 2
    tiles = lax.axis_size("tile")
    right_pairs = [(t, t + 1) for t in range(tiles) if t % GRID_W < GRID_W - 1]
    left_pairs = [(b, a) for a, b in right_pairs]
    down_pairs = [(t, t + GRID_W) for t in range(tiles - GRID_W)]
    up_pairs = [(b, a) for a, b in down_pairs]
    left = lax.ppermute(block[:, -halo:], "tile", right_pairs)
    right = lax.ppermute(block[:, :halo], "tile", left_pairs)
    wide = jnp.concatenate([left, block, right], axis=1)
    top = lax.ppermute(wide[-halo:], "tile", down_pairs)
    bottom = lax.ppermute(wide[:halo], "tile", up_pairs)
    return jnp.concatenate([top, wide, bottom], axis=0)


def summed(value):
    for axis in ("scene", "tile"):
        count = lax.axis_size(axis)
        bit = 1
        while bit < count:
            value = value + lax.ppermute(value, axis, [(d, d ^ bit) for d in range(count)])
            bit *= 2
    return value


def gelu_pair(hidden):
    inner_arg = SQRT_TWO_PI * (hidden + CUBIC * hidden * hidden * hidden)
    tangent = jnp.tanh(inner_arg)
    activated = 0.5 * hidden * (1.0 + tangent)
    derivative = 0.5 * (1.0 + tangent) + 0.5 * hidden * (1.0 - tangent * tangent) * SQRT_TWO_PI * (
        1.0 + 3.0 * CUBIC * hidden * hidden
    )
    return (activated, derivative)


def contract_rows(left_side, right_side):
    return lax.dot_general(
        left_side, right_side, (((0,), (0,)), ((), ())), preferred_element_type=jnp.float32
    )


def on_device(
    image,
    kernel,
    ln_gain,
    w_in,
    bias_in,
    w_out,
    layer_scale,
    grad_rows,
    return_pos,
    send_counts,
    send_offsets,
):
    scene_count = lax.axis_size("scene")
    tile_count = lax.axis_size("tile")
    peer_count = scene_count * tile_count
    height = image.shape[2]
    breadth = image.shape[3]
    channels = image.shape[4]
    tile_rows = height * breadth
    capacity = max(2, 2 * tile_rows // peer_count)
    starts = send_offsets[0]
    counts = send_counts[0]
    slot_index = jnp.arange(capacity, dtype=jnp.int32)
    filled = (slot_index[None, :] < counts[:, None]).reshape(-1)
    picked = (starts[:, None] + slot_index[None, :]).reshape(-1)
    own_slots = jnp.arange(grad_rows.shape[0], dtype=jnp.int32)
    chosen = (picked[:, None] == own_slots[None, :]) & filled[:, None]
    outgoing = jnp.dot(
        chosen.astype(jnp.bfloat16), grad_rows, preferred_element_type=jnp.float32
    ).astype(jnp.bfloat16)
    local_places = return_pos % tile_rows + 1
    targets = jnp.sum(jnp.where(chosen, local_places[None, :], 0), axis=1) - 1
    own_block = image[0, 0]
    padded = extend(own_block)
    outgoing, targets, padded = lax.optimization_barrier((outgoing, targets, padded))
    arrived, places = (
        lax.all_to_all(
            outgoing.reshape(peer_count, capacity, channels),
            ("scene", "tile"), split_axis=0, concat_axis=0, tiled=True,
        ),
        lax.all_to_all(
            targets.reshape(peer_count, capacity),
            ("scene", "tile"), split_axis=0, concat_axis=0, tiled=True,
        ),
    )
    arrived = arrived.reshape(-1, channels)
    places = places.reshape(-1)
    mixed_sum = lane_call(
        forward_body, (padded, kernel), (height, breadth, channels), jnp.float32, padded.shape
    ).reshape(tile_rows, channels)
    centre = mixed_sum - jnp.mean(mixed_sum, axis=-1, keepdims=True)
    inv_std = lax.rsqrt(jnp.mean(centre * centre, axis=-1, keepdims=True) + EPSILON)
    normed = centre * inv_std
    scaled = (normed * ln_gain).astype(jnp.bfloat16)
    hidden = jnp.dot(scaled, w_in, preferred_element_type=jnp.float32) + bias_in
    activated, derivative = gelu_pair(hidden)
    act_low = activated.astype(jnp.bfloat16)
    selector = (jnp.arange(tile_rows, dtype=jnp.int32)[:, None] == places[None, :]).astype(
        jnp.bfloat16
    )
    upstream = jnp.dot(selector, arrived, preferred_element_type=jnp.float32)
    branch_grad = (upstream * layer_scale).astype(jnp.bfloat16)
    act_grad = jnp.dot(branch_grad, w_out.T, preferred_element_type=jnp.float32)
    hidden_grad = (act_grad * derivative).astype(jnp.bfloat16)
    normed_grad = jnp.dot(hidden_grad, w_in.T, preferred_element_type=jnp.float32) * ln_gain
    mixed_grad = inv_std * (
        normed_grad
        - jnp.mean(normed_grad, axis=-1, keepdims=True)
        - normed * jnp.mean(normed_grad * normed, axis=-1, keepdims=True)
    )
    mixed_low = mixed_grad.astype(jnp.bfloat16).reshape(height, breadth, channels)
    grad_padded = extend(mixed_low)
    grad_input = lane_call(
        backward_body,
        (grad_padded, kernel, upstream.reshape(height, breadth, channels)),
        (height, breadth, channels),
        jnp.bfloat16,
        grad_padded.shape,
    )
    factor = 1.0 / math.sqrt(tile_rows * peer_count)
    kernel_factor = 1.0 / math.sqrt(GRID_W * GRID_W * tile_rows)
    term_out = contract_rows(act_low, branch_grad).astype(jnp.bfloat16)
    term_in = contract_rows(scaled, hidden_grad).astype(jnp.bfloat16)
    first_out, first_in = (
        lax.psum_scatter(term_out, "scene", scatter_dimension=0, tiled=True),
        lax.psum_scatter(term_in, "scene", scatter_dimension=0, tiled=True),
    )
    grad_out, grad_in = (
        lax.psum_scatter(first_out, "tile", scatter_dimension=0, tiled=True).astype(jnp.float32),
        lax.psum_scatter(first_in, "tile", scatter_dimension=0, tiled=True).astype(jnp.float32),
    )
    local_kernel = lane_call(
        terms_body, (mixed_low, padded), (KS, KS, channels), jnp.float32, padded.shape
    )
    grad_kernel = summed(local_kernel)
    return (
        grad_input.reshape(image.shape),
        grad_in * factor,
        grad_out * factor,
        grad_kernel * kernel_factor,
    )


def solution(mesh):
    placed = (
        P("scene", "tile", None, None, None),
        P(),
        P(),
        P(),
        P(),
        P(),
        P(),
        P(("scene", "tile"), None),
        P(("scene", "tile")),
        P(("scene", "tile"), None),
        P(("scene", "tile"), None),
    )
    return jax.shard_map(
        on_device,
        mesh=mesh,
        in_specs=placed,
        out_specs=(
            P("scene", "tile", None, None, None),
            P(("scene", "tile"), None),
            P(("scene", "tile"), None),
            P(),
        ),
        check_vma=False,
    )
```

```python
import functools
import math

import jax
import jax.numpy as jnp
from jax import lax
from jax.experimental import pallas as pl
from jax.experimental.pallas import tpu as pltpu
from jax.sharding import PartitionSpec as P

KS = 7
GRID_W = 4


EPSILON = 1e-06
SQRT_TWO_PI = 0.7978845608028654
CUBIC = 0.044715


LANES = 128
GROUP = 4


def widen(padded_ref, wide_ref):
    rows, cols = padded_ref.shape[0], padded_ref.shape[1]

    @pl.loop(0, rows)
    def _(row):
        wide_ref[row, pl.ds(0, cols), :] = padded_ref[row].astype(jnp.float32)


def conv_rows(wide_ref, kernel_ref, first, breadth, flip):
    sums = [jnp.zeros((breadth, LANES), jnp.float32) for _ in range(GROUP)]
    for col in range(KS):
        for row in range(GROUP + KS - 1):
            piece = wide_ref[first + row, pl.ds(col, breadth), :]
            for out in range(GROUP):
                tap = row - out
                if 0 <= tap < KS:
                    k_row, k_col = (KS - 1 - tap, KS - 1 - col) if flip else (tap, col)
                    sums[out] = sums[out] + kernel_ref[k_row, pl.ds(k_col, 1), :] * piece
    return sums


def forward_body(padded_ref, kernel_ref, out_ref, wide_ref):
    height, breadth = out_ref.shape[0], out_ref.shape[1]
    widen(padded_ref, wide_ref)

    @pl.loop(0, height // GROUP)
    def _(group):
        first = group * GROUP
        sums = conv_rows(wide_ref, kernel_ref, first, breadth, False)
        for out in range(GROUP):
            out_ref[first + out] = sums[out]


def backward_body(padded_ref, kernel_ref, up_ref, out_ref, wide_ref):
    height, breadth = out_ref.shape[0], out_ref.shape[1]
    widen(padded_ref, wide_ref)

    @pl.loop(0, height // GROUP)
    def _(group):
        first = group * GROUP
        sums = conv_rows(wide_ref, kernel_ref, first, breadth, True)
        for out in range(GROUP):
            out_ref[first + out] = (sums[out] + up_ref[first + out]).astype(out_ref.dtype)


def terms_body(grad_ref, padded_ref, out_ref, wide_ref):
    height, breadth = grad_ref.shape[0], grad_ref.shape[1]
    widen(padded_ref, wide_ref)
    for col in range(KS):

        def step(group, sums):
            first = group * GROUP
            sums = list(sums)
            grads = [grad_ref[first + out].astype(jnp.float32) for out in range(GROUP)]
            for row in range(GROUP + KS - 1):
                piece = wide_ref[first + row, pl.ds(col, breadth), :]
                for out in range(GROUP):
                    tap = row - out
                    if 0 <= tap < KS:
                        prod = (grads[out] * piece).reshape(breadth // 8, 8, LANES)
                        sums[tap] = sums[tap] + jnp.sum(prod, axis=0)
            return tuple(sums)

        zeros = tuple(jnp.zeros((8, LANES), jnp.float32) for _ in range(KS))
        sums = lax.fori_loop(0, height // GROUP, step, zeros)
        for tap in range(KS):
            out_ref[tap, pl.ds(col, 1), :] = jnp.sum(sums[tap], axis=0, keepdims=True)


def by_lanes(shape):
    return pl.BlockSpec(tuple(shape[:2]) + (LANES,), lambda lane: (0, 0, lane))


def lane_call(body, args, out_shape, out_type, wide):
    flops = 2 * KS * KS * wide[0] * wide[1] * out_shape[2]
    return pl.pallas_call(
        body,
        out_shape=jax.ShapeDtypeStruct(out_shape, out_type),
        grid=(out_shape[2] // LANES,),
        in_specs=[by_lanes(arg.shape) for arg in args],
        out_specs=by_lanes(out_shape),
        scratch_shapes=[pltpu.VMEM((wide[0], -(-wide[1] // 8) * 8, LANES), jnp.float32)],
        compiler_params=pltpu.CompilerParams(vmem_limit_bytes=24 * 2**20),
        cost_estimate=pl.CostEstimate(flops=flops * 100, bytes_accessed=40 * 2**20, transcendentals=0),
    )(*args)


def extend(block):
    halo = KS // 2
    tiles = lax.axis_size("tile")
    right_pairs = [(t, t + 1) for t in range(tiles) if t % GRID_W < GRID_W - 1]
    left_pairs = [(b, a) for a, b in right_pairs]
    down_pairs = [(t, t + GRID_W) for t in range(tiles - GRID_W)]
    up_pairs = [(b, a) for a, b in down_pairs]
    left = lax.ppermute(block[:, -halo:], "tile", right_pairs)
    right = lax.ppermute(block[:, :halo], "tile", left_pairs)
    wide = jnp.concatenate([left, block, right], axis=1)
    top = lax.ppermute(wide[-halo:], "tile", down_pairs)
    bottom = lax.ppermute(wide[:halo], "tile", up_pairs)
    return jnp.concatenate([top, wide, bottom], axis=0)


MESH = pl.DeviceIdType.MESH
SIDES = [(r, c) for r in (-1, 0, 1) for c in (-1, 0, 1) if (r, c) != (0, 0)]


def bits_of(count):
    return [1 << k for k in reversed(range(count.bit_length() - 1))]


def place_of(scenes, tiles):
    return [("scene", bit) for bit in bits_of(scenes)] + [("tile", bit) for bit in bits_of(tiles)]


def exchange_body(
    scenes, tiles, factor, kernel_factor,
    in_ref, out_ref, grad_ref, first_ref, last_ref, local_ref,
    w_in_ref, w_out_ref, kernel_ref, *rest,
):
    places = place_of(scenes, tiles)
    steps = len(places)
    halos = rest[:8]
    rest = rest[8:]
    got_in, got_out = rest[:steps], rest[steps : 2 * steps]
    got_kernel, sent_kernel, send_sems, recv_sems, halo_send, halo_recv = rest[2 * steps :]
    me = {"scene": lax.axis_index("scene"), "tile": lax.axis_index("tile")}
    scene_bits = [p for p in places if p[0] == "scene"][::-1]
    tile_bits = [p for p in places if p[0] == "tile"][::-1]
    order_in = scene_bits + tile_bits
    order_out = scene_bits[:1] + tile_bits + scene_bits[1:]

    def half(place):
        return lax.rem(me[place[0]] // place[1], 2)

    def partner(place):
        return {place[0]: me[place[0]] + place[1] * (1 - 2 * half(place))}

    grid_row, grid_col = me["tile"] // GRID_W, lax.rem(me["tile"], GRID_W)

    def present(side):
        row, col = grid_row + side[0], grid_col + side[1]
        return (row >= 0) & (row < tiles // GRID_W) & (col >= 0) & (col < GRID_W)

    def neighbour(side):
        return {"tile": me["tile"] + side[0] * GRID_W + side[1]}

    barrier = pltpu.get_barrier_semaphore()
    for place in places:
        pl.semaphore_signal(barrier, inc=1, device_id=partner(place), device_id_type=MESH)
    for side in SIDES:

        @pl.when(present(side))
        def _():
            pl.semaphore_signal(barrier, inc=1, device_id=neighbour(side), device_id_type=MESH)

    pl.semaphore_wait(
        barrier, steps + sum(jnp.where(present(side), 1, 0).astype(jnp.int32) for side in SIDES)
    )

    def position(order, step):
        left = [p for p in places if p not in order[:step]]
        return left.index(order[step])

    def weight_copy(which, order, source, got, step):
        place = order[step]
        pos = position(order, step)
        src = source if step == 0 else got[step - 1]
        return pltpu.make_async_remote_copy(
            src_ref=src.at[(slice(None),) * pos + (1 - half(place),)],
            dst_ref=got[step],
            send_sem=send_sems.at[which, step],
            recv_sem=recv_sems.at[which, step],
            device_id=partner(place),
            device_id_type=MESH,
        )

    def weight_add(order, source, got, step, result):
        pos = position(order, step)
        src = source if step == 0 else got[step - 1]
        dims = steps - 1 - step
        mine = half(order[step])

        def one(chunk, carry):
            index = tuple(lax.rem(chunk // (1 << (dims - 1 - d)), 2) for d in range(dims))
            held = index[:pos] + (mine,) + index[pos:]
            total = got[step][index].astype(jnp.float32) + src[held].astype(jnp.float32)
            got[step][index] = total.astype(jnp.bfloat16)
            return carry

        if dims:
            lax.fori_loop(0, 1 << dims, one, 0)
        else:
            total = got[step][...].astype(jnp.float32) + src[mine].astype(jnp.float32)
            result[...] = total * factor

    def kernel_copy(step):
        return pltpu.make_async_remote_copy(
            src_ref=sent_kernel.at[step],
            dst_ref=got_kernel.at[step],
            send_sem=send_sems.at[2, step],
            recv_sem=recv_sems.at[2, step],
            device_id=partner(order_in[step]),
            device_id_type=MESH,
        )

    def halo_copy(number):
        row, col = SIDES[number]
        source = {-1: first_ref, 0: grad_ref, 1: last_ref}[col]
        width = KS // 2
        if row == -1:
            source = source.at[pl.ds(0, width)]
        elif row == 1:
            source = source.at[pl.ds(grad_ref.shape[0] - width, width)]
        return pltpu.make_async_remote_copy(
            src_ref=source,
            dst_ref=halos[SIDES.index((-row, -col))],
            send_sem=halo_send.at[number],
            recv_sem=halo_recv.at[SIDES.index((-row, -col))],
            device_id=neighbour((row, col)),
            device_id_type=MESH,
        )

    def halo_arrival(number):
        row, col = SIDES[number]
        return pltpu.make_async_remote_copy(
            src_ref=halos[number],
            dst_ref=halos[number],
            send_sem=halo_send.at[number],
            recv_sem=halo_recv.at[number],
            device_id=neighbour((row, col)),
            device_id_type=MESH,
        )

    for number in range(8):

        @pl.when(present(SIDES[number]))
        def _():
            halo_copy(number).start()

    copies_in = [weight_copy(0, order_in, in_ref, got_in, step) for step in range(steps)]
    copies_out = [weight_copy(1, order_out, out_ref, got_out, step) for step in range(steps)]
    copies_kernel = [kernel_copy(step) for step in range(steps)]
    copies_in[0].start()
    copies_out[0].start()
    sent_kernel[0] = local_ref[...]
    copies_kernel[0].start()
    for step in range(steps):
        later = step < steps - 1
        copies_in[step].wait_recv()
        weight_add(order_in, in_ref, got_in, step, w_in_ref)
        if later:
            copies_in[step + 1].start()
        copies_out[step].wait_recv()
        weight_add(order_out, out_ref, got_out, step, w_out_ref)
        if later:
            copies_out[step + 1].start()
        copies_kernel[step].wait_recv()
        if later:
            sent_kernel[step + 1] = sent_kernel[step] + got_kernel[step]
            copies_kernel[step + 1].start()
        else:
            kernel_ref[...] = (sent_kernel[step] + got_kernel[step]) * kernel_factor
    for number in range(8):

        @pl.when(present(SIDES[number]))
        def _():
            halo_copy(number).wait_send()
            halo_arrival(number).wait_recv()

        @pl.when(jnp.logical_not(present(SIDES[number])))
        def _():
            halos[number][...] = jnp.zeros(halos[number].shape, halos[number].dtype)

    for step in range(steps):
        copies_in[step].wait_send()
        copies_out[step].wait_send()
        copies_kernel[step].wait_send()


def exchange(term_in, term_out, grad, local_kernel, factor, kernel_factor):
    scenes, tiles = lax.axis_size("scene"), lax.axis_size("tile")
    peers = scenes * tiles
    steps = peers.bit_length() - 1
    halo = KS // 2
    height, breadth, channels = grad.shape
    cut_in = (term_in.shape[0] // peers, term_in.shape[1])
    cut_out = (term_out.shape[0] // peers, term_out.shape[1])
    tall = {-1: halo, 0: height, 1: halo}
    broad = {-1: halo, 0: breadth, 1: halo}
    whole = pl.BlockSpec(memory_space=pltpu.VMEM)
    results = pl.pallas_call(
        functools.partial(exchange_body, scenes, tiles, factor, kernel_factor),
        out_shape=[
            jax.ShapeDtypeStruct(cut_in, jnp.float32),
            jax.ShapeDtypeStruct(cut_out, jnp.float32),
            jax.ShapeDtypeStruct(local_kernel.shape, jnp.float32),
        ]
        + [jax.ShapeDtypeStruct((tall[r], broad[c], channels), jnp.bfloat16) for r, c in SIDES],
        in_specs=[whole] * 6,
        out_specs=[whole] * 11,
        scratch_shapes=[
            pltpu.VMEM((2,) * (steps - 1 - k) + cut_in, jnp.bfloat16) for k in range(steps)
        ]
        + [pltpu.VMEM((2,) * (steps - 1 - k) + cut_out, jnp.bfloat16) for k in range(steps)]
        + [
            pltpu.VMEM((steps,) + local_kernel.shape, jnp.float32),
            pltpu.VMEM((steps,) + local_kernel.shape, jnp.float32),
            pltpu.SemaphoreType.DMA((3, steps)),
            pltpu.SemaphoreType.DMA((3, steps)),
            pltpu.SemaphoreType.DMA((8,)),
            pltpu.SemaphoreType.DMA((8,)),
        ],
        compiler_params=pltpu.CompilerParams(
            collective_id=0, has_side_effects=True, vmem_limit_bytes=48 * 2**20
        ),
    )(
        term_in.reshape((2,) * steps + cut_in),
        term_out.reshape((2,) * steps + cut_out),
        grad,
        grad[:, :halo],
        grad[:, -halo:],
        local_kernel,
    )
    w_in, w_out, kernel = results[:3]
    around = dict(zip(SIDES, results[3:]))
    around[(0, 0)] = grad
    bands = [jnp.concatenate([around[(r, c)] for c in (-1, 0, 1)], axis=1) for r in (-1, 0, 1)]
    return w_in, w_out, kernel, jnp.concatenate(bands, axis=0)


def gelu_pair(hidden):
    inner_arg = SQRT_TWO_PI * (hidden + CUBIC * hidden * hidden * hidden)
    tangent = jnp.tanh(inner_arg)
    activated = 0.5 * hidden * (1.0 + tangent)
    derivative = 0.5 * (1.0 + tangent) + 0.5 * hidden * (1.0 - tangent * tangent) * SQRT_TWO_PI * (
        1.0 + 3.0 * CUBIC * hidden * hidden
    )
    return (activated, derivative)


def contract_rows(left_side, right_side):
    return lax.dot_general(
        left_side, right_side, (((0,), (0,)), ((), ())), preferred_element_type=jnp.float32
    )


def on_device(
    image,
    kernel,
    ln_gain,
    w_in,
    bias_in,
    w_out,
    layer_scale,
    grad_rows,
    return_pos,
    send_counts,
    send_offsets,
):
    scene_count = lax.axis_size("scene")
    tile_count = lax.axis_size("tile")
    peer_count = scene_count * tile_count
    height = image.shape[2]
    breadth = image.shape[3]
    channels = image.shape[4]
    tile_rows = height * breadth
    capacity = max(2, 2 * tile_rows // peer_count)
    starts = send_offsets[0]
    counts = send_counts[0]
    slot_index = jnp.arange(capacity, dtype=jnp.int32)
    filled = (slot_index[None, :] < counts[:, None]).reshape(-1)
    picked = (starts[:, None] + slot_index[None, :]).reshape(-1)
    own_slots = jnp.arange(grad_rows.shape[0], dtype=jnp.int32)
    chosen = (picked[:, None] == own_slots[None, :]) & filled[:, None]
    outgoing = jnp.dot(
        chosen.astype(jnp.bfloat16), grad_rows, preferred_element_type=jnp.float32
    ).astype(jnp.bfloat16)
    local_places = return_pos % tile_rows + 1
    targets = jnp.sum(jnp.where(chosen, local_places[None, :], 0), axis=1) - 1
    own_block = image[0, 0]
    padded = extend(own_block)
    outgoing, targets, padded = lax.optimization_barrier((outgoing, targets, padded))
    arrived, places = (
        lax.all_to_all(
            outgoing.reshape(peer_count, capacity, channels),
            ("scene", "tile"), split_axis=0, concat_axis=0, tiled=True,
        ),
        lax.all_to_all(
            targets.reshape(peer_count, capacity),
            ("scene", "tile"), split_axis=0, concat_axis=0, tiled=True,
        ),
    )
    arrived = arrived.reshape(-1, channels)
    places = places.reshape(-1)
    mixed_sum = lane_call(
        forward_body, (padded, kernel), (height, breadth, channels), jnp.float32, padded.shape
    ).reshape(tile_rows, channels)
    centre = mixed_sum - jnp.mean(mixed_sum, axis=-1, keepdims=True)
    inv_std = lax.rsqrt(jnp.mean(centre * centre, axis=-1, keepdims=True) + EPSILON)
    normed = centre * inv_std
    scaled = (normed * ln_gain).astype(jnp.bfloat16)
    hidden = jnp.dot(scaled, w_in, preferred_element_type=jnp.float32) + bias_in
    activated, derivative = gelu_pair(hidden)
    act_low = activated.astype(jnp.bfloat16)
    selector = (jnp.arange(tile_rows, dtype=jnp.int32)[:, None] == places[None, :]).astype(
        jnp.bfloat16
    )
    upstream = jnp.dot(selector, arrived, preferred_element_type=jnp.float32)
    branch_grad = (upstream * layer_scale).astype(jnp.bfloat16)
    act_grad = jnp.dot(branch_grad, w_out.T, preferred_element_type=jnp.float32)
    hidden_grad = (act_grad * derivative).astype(jnp.bfloat16)
    normed_grad = jnp.dot(hidden_grad, w_in.T, preferred_element_type=jnp.float32) * ln_gain
    mixed_grad = inv_std * (
        normed_grad
        - jnp.mean(normed_grad, axis=-1, keepdims=True)
        - normed * jnp.mean(normed_grad * normed, axis=-1, keepdims=True)
    )
    mixed_low = mixed_grad.astype(jnp.bfloat16).reshape(height, breadth, channels)
    factor = 1.0 / math.sqrt(tile_rows * peer_count)
    kernel_factor = 1.0 / math.sqrt(GRID_W * GRID_W * tile_rows)
    term_out = contract_rows(act_low, branch_grad).astype(jnp.bfloat16)
    term_in = contract_rows(scaled, hidden_grad).astype(jnp.bfloat16)
    local_kernel = lane_call(
        terms_body, (mixed_low, padded), (KS, KS, channels), jnp.float32, padded.shape
    )
    grad_in, grad_out, grad_kernel, grad_padded = exchange(
        term_in, term_out, mixed_low, local_kernel, factor, kernel_factor
    )
    grad_input = lane_call(
        backward_body,
        (grad_padded, kernel, upstream.reshape(height, breadth, channels)),
        (height, breadth, channels),
        jnp.bfloat16,
        grad_padded.shape,
    )
    return grad_input.reshape(image.shape), grad_in, grad_out, grad_kernel


def solution(mesh):
    placed = (
        P("scene", "tile", None, None, None),
        P(),
        P(),
        P(),
        P(),
        P(),
        P(),
        P(("scene", "tile"), None),
        P(("scene", "tile")),
        P(("scene", "tile"), None),
        P(("scene", "tile"), None),
    )
    return jax.shard_map(
        on_device,
        mesh=mesh,
        in_specs=placed,
        out_specs=(
            P("scene", "tile", None, None, None),
            P(("scene", "tile"), None),
            P(("scene", "tile"), None),
            P(),
        ),
        check_vma=False,
    )
```

```python
import functools
import math

import jax
import jax.numpy as jnp
from jax import lax
from jax.experimental import pallas as pl
from jax.experimental.pallas import tpu as pltpu
from jax.sharding import PartitionSpec as P

KS = 7
GRID_W = 4


EPSILON = 1e-06
SQRT_TWO_PI = 0.7978845608028654
CUBIC = 0.044715


LANES = 128
GROUP = 4


def widen(padded_ref, wide_ref):
    rows, cols = padded_ref.shape[0], padded_ref.shape[1]

    @pl.loop(0, rows)
    def _(row):
        wide_ref[row, pl.ds(0, cols), :] = padded_ref[row].astype(jnp.float32)


def conv_rows(wide_ref, kernel_ref, first, breadth, flip):
    sums = [jnp.zeros((breadth, LANES), jnp.float32) for _ in range(GROUP)]
    for col in range(KS):
        for row in range(GROUP + KS - 1):
            piece = wide_ref[first + row, pl.ds(col, breadth), :]
            for out in range(GROUP):
                tap = row - out
                if 0 <= tap < KS:
                    k_row, k_col = (KS - 1 - tap, KS - 1 - col) if flip else (tap, col)
                    sums[out] = sums[out] + kernel_ref[k_row, pl.ds(k_col, 1), :] * piece
    return sums


def forward_body(padded_ref, kernel_ref, out_ref, wide_ref):
    height, breadth = out_ref.shape[0], out_ref.shape[1]
    widen(padded_ref, wide_ref)

    @pl.loop(0, height // GROUP)
    def _(group):
        first = group * GROUP
        sums = conv_rows(wide_ref, kernel_ref, first, breadth, False)
        for out in range(GROUP):
            out_ref[first + out] = sums[out]


def backward_part(wide_ref, kernel_ref, up_ref, out_ref):
    height, breadth = out_ref.shape[0], out_ref.shape[1]

    @pl.loop(0, height // GROUP)
    def _(group):
        first = group * GROUP
        sums = conv_rows(wide_ref, kernel_ref, first, breadth, True)
        for out in range(GROUP):
            out_ref[first + out] = (sums[out] + up_ref[first + out]).astype(out_ref.dtype)


def terms_body(grad_ref, padded_ref, out_ref, wide_ref):
    height, breadth = grad_ref.shape[0], grad_ref.shape[1]
    widen(padded_ref, wide_ref)
    for col in range(KS):

        def step(group, sums):
            first = group * GROUP
            sums = list(sums)
            grads = [grad_ref[first + out].astype(jnp.float32) for out in range(GROUP)]
            for row in range(GROUP + KS - 1):
                piece = wide_ref[first + row, pl.ds(col, breadth), :]
                for out in range(GROUP):
                    tap = row - out
                    if 0 <= tap < KS:
                        prod = (grads[out] * piece).reshape(breadth // 8, 8, LANES)
                        sums[tap] = sums[tap] + jnp.sum(prod, axis=0)
            return tuple(sums)

        zeros = tuple(jnp.zeros((8, LANES), jnp.float32) for _ in range(KS))
        sums = lax.fori_loop(0, height // GROUP, step, zeros)
        for tap in range(KS):
            out_ref[tap, pl.ds(col, 1), :] = jnp.sum(sums[tap], axis=0, keepdims=True)


def by_lanes(shape):
    return pl.BlockSpec(tuple(shape[:2]) + (LANES,), lambda lane: (0, 0, lane))


def lane_call(body, args, out_shape, out_type, wide):
    flops = 2 * KS * KS * wide[0] * wide[1] * out_shape[2]
    return pl.pallas_call(
        body,
        out_shape=jax.ShapeDtypeStruct(out_shape, out_type),
        grid=(out_shape[2] // LANES,),
        in_specs=[by_lanes(arg.shape) for arg in args],
        out_specs=by_lanes(out_shape),
        scratch_shapes=[pltpu.VMEM((wide[0], -(-wide[1] // 8) * 8, LANES), jnp.float32)],
        compiler_params=pltpu.CompilerParams(vmem_limit_bytes=24 * 2**20),
        cost_estimate=pl.CostEstimate(flops=flops * 100, bytes_accessed=40 * 2**20, transcendentals=0),
    )(*args)


MESH = pl.DeviceIdType.MESH
SIDES = [(r, c) for r in (-1, 0, 1) for c in (-1, 0, 1) if (r, c) != (0, 0)]


def bits_of(count):
    return [1 << k for k in reversed(range(count.bit_length() - 1))]


def place_of(scenes, tiles):
    return [("scene", bit) for bit in bits_of(scenes)] + [("tile", bit) for bit in bits_of(tiles)]


class Halo:
    def __init__(self, tiles, block_ref, first_ref, last_ref, pieces, send, recv):
        tile = lax.axis_index("tile")
        self.tile, self.pieces, self.send, self.recv = tile, pieces, send, recv
        self.block, self.first, self.last = block_ref, first_ref, last_ref
        row, col = tile // GRID_W, lax.rem(tile, GRID_W)
        self.there = [
            (row + r >= 0) & (row + r < tiles // GRID_W) & (col + c >= 0) & (col + c < GRID_W)
            for r, c in SIDES
        ]

    def neighbour(self, number):
        row, col = SIDES[number]
        return {"tile": self.tile + row * GRID_W + col}

    def greet(self, barrier):
        for number in range(8):

            @pl.when(self.there[number])
            def _():
                pl.semaphore_signal(
                    barrier, inc=1, device_id=self.neighbour(number), device_id_type=MESH
                )

        return sum(jnp.where(there, 1, 0).astype(jnp.int32) for there in self.there)

    def copy(self, number):
        row, col = SIDES[number]
        source = {-1: self.first, 0: self.block, 1: self.last}[col]
        width = KS // 2
        if row == -1:
            source = source.at[pl.ds(0, width)]
        elif row == 1:
            source = source.at[pl.ds(self.block.shape[0] - width, width)]
        landing = SIDES.index((-row, -col))
        return pltpu.make_async_remote_copy(
            src_ref=source,
            dst_ref=self.pieces[landing],
            send_sem=self.send.at[number],
            recv_sem=self.recv.at[landing],
            device_id=self.neighbour(number),
            device_id_type=MESH,
        )

    def arrival(self, number):
        return pltpu.make_async_remote_copy(
            src_ref=self.pieces[number],
            dst_ref=self.pieces[number],
            send_sem=self.send.at[number],
            recv_sem=self.recv.at[number],
            device_id=self.neighbour(number),
            device_id_type=MESH,
        )

    def start(self):
        for number in range(8):

            @pl.when(self.there[number])
            def _():
                self.copy(number).start()

    def finish(self):
        for number in range(8):
            piece = self.pieces[number]

            @pl.when(self.there[number])
            def _():
                self.copy(number).wait_send()
                self.arrival(number).wait_recv()

            @pl.when(jnp.logical_not(self.there[number]))
            def _():
                piece[...] = jnp.zeros(piece.shape, piece.dtype)

    def assemble(self, lanes, wide_ref):
        height, breadth = self.block.shape[0], self.block.shape[1]
        width = KS // 2
        parts = dict(zip(SIDES, self.pieces))
        parts[(0, 0)] = self.block
        for row, first, count in ((-1, 0, width), (0, width, height), (1, width + height, width)):

            @pl.loop(0, count)
            def _(line):
                for col, place, size in (
                    (-1, 0, width), (0, width, breadth), (1, width + breadth, width)
                ):
                    wide_ref[first + line, pl.ds(place, size), :] = parts[(row, col)][
                        line, :, lanes
                    ].astype(jnp.float32)


def halo_shapes(shape):
    halo = KS // 2
    tall = {-1: halo, 0: shape[0], 1: halo}
    broad = {-1: halo, 0: shape[1], 1: halo}
    return [(tall[r], broad[c], shape[2]) for r, c in SIDES]


def halo_body(tiles, block_ref, first_ref, last_ref, *rest):
    halo = Halo(tiles, block_ref, first_ref, last_ref, rest[:8], rest[8], rest[9])
    barrier = pltpu.get_barrier_semaphore()
    pl.semaphore_wait(barrier, halo.greet(barrier))
    halo.start()
    halo.finish()


def extend(block):
    width = KS // 2
    whole = pl.BlockSpec(memory_space=pltpu.VMEM)
    results = pl.pallas_call(
        functools.partial(halo_body, lax.axis_size("tile")),
        out_shape=[jax.ShapeDtypeStruct(shape, jnp.bfloat16) for shape in halo_shapes(block.shape)],
        in_specs=[whole] * 3,
        out_specs=[whole] * 8,
        scratch_shapes=[pltpu.SemaphoreType.DMA((8,)), pltpu.SemaphoreType.DMA((8,))],
        compiler_params=pltpu.CompilerParams(
            collective_id=1, has_side_effects=True, vmem_limit_bytes=16 * 2**20
        ),
    )(block, block[:, :width], block[:, -width:])
    around = dict(zip(SIDES, results))
    around[(0, 0)] = block
    bands = [jnp.concatenate([around[(r, c)] for c in (-1, 0, 1)], axis=1) for r in (-1, 0, 1)]
    return jnp.concatenate(bands, axis=0)


def exchange_body(
    scenes, tiles, factor, kernel_factor,
    in_ref, out_ref, grad_ref, first_ref, last_ref, padded_ref, taps_ref, up_ref,
    w_in_ref, w_out_ref, kernel_ref, image_ref, *rest,
):
    places = place_of(scenes, tiles)
    steps = len(places)
    halos = rest[:8]
    rest = rest[8:]
    got_in, got_out = rest[:steps], rest[steps : 2 * steps]
    got_kernel, sent_kernel, send_sems, recv_sems, halo_send, halo_recv, wide_ref = rest[2 * steps :]
    halo = Halo(tiles, grad_ref, first_ref, last_ref, halos, halo_send, halo_recv)
    me = {"scene": lax.axis_index("scene"), "tile": lax.axis_index("tile")}
    scene_bits = [p for p in places if p[0] == "scene"][::-1]
    tile_bits = [p for p in places if p[0] == "tile"][::-1]
    order_in = scene_bits + tile_bits
    order_out = scene_bits[:1] + tile_bits + scene_bits[1:]

    def half(place):
        return lax.rem(me[place[0]] // place[1], 2)

    def partner(place):
        return {place[0]: me[place[0]] + place[1] * (1 - 2 * half(place))}

    barrier = pltpu.get_barrier_semaphore()
    for place in places:
        pl.semaphore_signal(barrier, inc=1, device_id=partner(place), device_id_type=MESH)
    pl.semaphore_wait(barrier, steps + halo.greet(barrier))

    def position(order, step):
        left = [p for p in places if p not in order[:step]]
        return left.index(order[step])

    def weight_copy(which, order, source, got, step):
        place = order[step]
        pos = position(order, step)
        src = source if step == 0 else got[step - 1]
        return pltpu.make_async_remote_copy(
            src_ref=src.at[(slice(None),) * pos + (1 - half(place),)],
            dst_ref=got[step],
            send_sem=send_sems.at[which, step],
            recv_sem=recv_sems.at[which, step],
            device_id=partner(place),
            device_id_type=MESH,
        )

    def weight_add(order, source, got, step, result):
        pos = position(order, step)
        src = source if step == 0 else got[step - 1]
        dims = steps - 1 - step
        mine = half(order[step])

        def one(chunk, carry):
            index = tuple(lax.rem(chunk // (1 << (dims - 1 - d)), 2) for d in range(dims))
            held = index[:pos] + (mine,) + index[pos:]
            total = got[step][index].astype(jnp.float32) + src[held].astype(jnp.float32)
            got[step][index] = total.astype(jnp.bfloat16)
            return carry

        if dims:
            lax.fori_loop(0, 1 << dims, one, 0)
        else:
            total = got[step][...].astype(jnp.float32) + src[mine].astype(jnp.float32)
            result[...] = total * factor

    def kernel_copy(step):
        return pltpu.make_async_remote_copy(
            src_ref=sent_kernel.at[step],
            dst_ref=got_kernel.at[step],
            send_sem=send_sems.at[2, step],
            recv_sem=recv_sems.at[2, step],
            device_id=partner(order_in[step]),
            device_id_type=MESH,
        )

    def each_lane(work):
        @pl.loop(0, grad_ref.shape[2] // LANES)
        def _(lane):
            work(pl.ds(pl.multiple_of(lane * LANES, LANES), LANES))

    def kernel_part(lanes):
        terms_body(
            grad_ref.at[:, :, lanes],
            padded_ref.at[:, :, lanes],
            sent_kernel.at[0, :, :, lanes],
            wide_ref,
        )

    def image_part(lanes):
        halo.assemble(lanes, wide_ref)
        backward_part(
            wide_ref, taps_ref.at[:, :, lanes], up_ref.at[:, :, lanes], image_ref.at[:, :, lanes]
        )

    copies_in = [weight_copy(0, order_in, in_ref, got_in, step) for step in range(steps)]
    copies_out = [weight_copy(1, order_out, out_ref, got_out, step) for step in range(steps)]
    copies_kernel = [kernel_copy(step) for step in range(steps)]
    copies_in[0].start()
    copies_out[0].start()
    halo.start()
    each_lane(kernel_part)
    copies_kernel[0].start()
    for step in range(steps):
        later = step < steps - 1
        copies_in[step].wait_recv()
        weight_add(order_in, in_ref, got_in, step, w_in_ref)
        if later:
            copies_in[step + 1].start()
        copies_out[step].wait_recv()
        weight_add(order_out, out_ref, got_out, step, w_out_ref)
        if later:
            copies_out[step + 1].start()
        copies_kernel[step].wait_recv()
        if later:
            sent_kernel[step + 1] = sent_kernel[step] + got_kernel[step]
            copies_kernel[step + 1].start()
        else:
            kernel_ref[...] = (sent_kernel[step] + got_kernel[step]) * kernel_factor
        if step == 0:
            halo.finish()
            each_lane(image_part)
    for step in range(steps):
        copies_in[step].wait_send()
        copies_out[step].wait_send()
        copies_kernel[step].wait_send()


def exchange(term_in, term_out, grad, padded, kernel, upstream, factor, kernel_factor):
    scenes, tiles = lax.axis_size("scene"), lax.axis_size("tile")
    peers = scenes * tiles
    steps = peers.bit_length() - 1
    halo = KS // 2
    height, breadth, channels = grad.shape
    cut_in = (term_in.shape[0] // peers, term_in.shape[1])
    cut_out = (term_out.shape[0] // peers, term_out.shape[1])
    whole = pl.BlockSpec(memory_space=pltpu.VMEM)
    results = pl.pallas_call(
        functools.partial(exchange_body, scenes, tiles, factor, kernel_factor),
        out_shape=[
            jax.ShapeDtypeStruct(cut_in, jnp.float32),
            jax.ShapeDtypeStruct(cut_out, jnp.float32),
            jax.ShapeDtypeStruct(kernel.shape, jnp.float32),
            jax.ShapeDtypeStruct(grad.shape, jnp.bfloat16),
        ],
        in_specs=[whole] * 8,
        out_specs=[whole] * 4,
        scratch_shapes=[pltpu.VMEM(shape, jnp.bfloat16) for shape in halo_shapes(grad.shape)]
        + [
            pltpu.VMEM((2,) * (steps - 1 - k) + cut_in, jnp.bfloat16) for k in range(steps)
        ]
        + [pltpu.VMEM((2,) * (steps - 1 - k) + cut_out, jnp.bfloat16) for k in range(steps)]
        + [
            pltpu.VMEM((steps,) + kernel.shape, jnp.float32),
            pltpu.VMEM((steps,) + kernel.shape, jnp.float32),
            pltpu.SemaphoreType.DMA((3, steps)),
            pltpu.SemaphoreType.DMA((3, steps)),
            pltpu.SemaphoreType.DMA((8,)),
            pltpu.SemaphoreType.DMA((8,)),
            pltpu.VMEM((height + 2 * halo, -(-(breadth + 2 * halo) // 8) * 8, LANES), jnp.float32),
        ],
        compiler_params=pltpu.CompilerParams(
            collective_id=0, has_side_effects=True, vmem_limit_bytes=48 * 2**20
        ),
    )(
        term_in.reshape((2,) * steps + cut_in),
        term_out.reshape((2,) * steps + cut_out),
        grad,
        grad[:, :halo],
        grad[:, -halo:],
        padded,
        kernel,
        upstream,
    )
    return results


def gelu_pair(hidden):
    inner_arg = SQRT_TWO_PI * (hidden + CUBIC * hidden * hidden * hidden)
    tangent = jnp.tanh(inner_arg)
    activated = 0.5 * hidden * (1.0 + tangent)
    derivative = 0.5 * (1.0 + tangent) + 0.5 * hidden * (1.0 - tangent * tangent) * SQRT_TWO_PI * (
        1.0 + 3.0 * CUBIC * hidden * hidden
    )
    return (activated, derivative)


def contract_rows(left_side, right_side):
    return lax.dot_general(
        left_side, right_side, (((0,), (0,)), ((), ())), preferred_element_type=jnp.float32
    )


def on_device(
    image,
    kernel,
    ln_gain,
    w_in,
    bias_in,
    w_out,
    layer_scale,
    grad_rows,
    return_pos,
    send_counts,
    send_offsets,
):
    scene_count = lax.axis_size("scene")
    tile_count = lax.axis_size("tile")
    peer_count = scene_count * tile_count
    height = image.shape[2]
    breadth = image.shape[3]
    channels = image.shape[4]
    tile_rows = height * breadth
    capacity = max(2, 2 * tile_rows // peer_count)
    starts = send_offsets[0]
    counts = send_counts[0]
    slot_index = jnp.arange(capacity, dtype=jnp.int32)
    filled = (slot_index[None, :] < counts[:, None]).reshape(-1)
    picked = (starts[:, None] + slot_index[None, :]).reshape(-1)
    own_slots = jnp.arange(grad_rows.shape[0], dtype=jnp.int32)
    chosen = (picked[:, None] == own_slots[None, :]) & filled[:, None]
    outgoing = jnp.dot(
        chosen.astype(jnp.bfloat16), grad_rows, preferred_element_type=jnp.float32
    ).astype(jnp.bfloat16)
    local_places = return_pos % tile_rows + 1
    targets = jnp.sum(jnp.where(chosen, local_places[None, :], 0), axis=1) - 1
    own_block = image[0, 0]
    padded = extend(own_block)
    outgoing, padded = lax.optimization_barrier((outgoing, padded))
    arrived = lax.all_to_all(
        outgoing.reshape(peer_count, capacity, channels),
        ("scene", "tile"), split_axis=0, concat_axis=0, tiled=True,
    )
    everyone = lax.all_gather(targets.reshape(1, peer_count * capacity), ("scene", "tile"), tiled=True)
    mine = lax.axis_index(("scene", "tile")) * capacity
    places = lax.dynamic_slice_in_dim(everyone, mine, capacity, axis=1)
    arrived = arrived.reshape(-1, channels)
    places = places.reshape(-1)
    mixed_sum = lane_call(
        forward_body, (padded, kernel), (height, breadth, channels), jnp.float32, padded.shape
    ).reshape(tile_rows, channels)
    centre = mixed_sum - jnp.mean(mixed_sum, axis=-1, keepdims=True)
    inv_std = lax.rsqrt(jnp.mean(centre * centre, axis=-1, keepdims=True) + EPSILON)
    normed = centre * inv_std
    scaled = (normed * ln_gain).astype(jnp.bfloat16)
    hidden = jnp.dot(scaled, w_in, preferred_element_type=jnp.float32) + bias_in
    activated, derivative = gelu_pair(hidden)
    act_low = activated.astype(jnp.bfloat16)
    selector = (jnp.arange(tile_rows, dtype=jnp.int32)[:, None] == places[None, :]).astype(
        jnp.bfloat16
    )
    upstream = jnp.dot(selector, arrived, preferred_element_type=jnp.float32)
    branch_grad = (upstream * layer_scale).astype(jnp.bfloat16)
    act_grad = jnp.dot(branch_grad, w_out.T, preferred_element_type=jnp.float32)
    hidden_grad = (act_grad * derivative).astype(jnp.bfloat16)
    normed_grad = jnp.dot(hidden_grad, w_in.T, preferred_element_type=jnp.float32) * ln_gain
    mixed_grad = inv_std * (
        normed_grad
        - jnp.mean(normed_grad, axis=-1, keepdims=True)
        - normed * jnp.mean(normed_grad * normed, axis=-1, keepdims=True)
    )
    mixed_low = mixed_grad.astype(jnp.bfloat16).reshape(height, breadth, channels)
    factor = 1.0 / math.sqrt(tile_rows * peer_count)
    kernel_factor = 1.0 / math.sqrt(GRID_W * GRID_W * tile_rows)
    term_out = contract_rows(act_low, branch_grad).astype(jnp.bfloat16)
    term_in = contract_rows(scaled, hidden_grad).astype(jnp.bfloat16)
    grad_in, grad_out, grad_kernel, grad_input = exchange(
        term_in,
        term_out,
        mixed_low,
        padded,
        kernel,
        upstream.reshape(height, breadth, channels),
        factor,
        kernel_factor,
    )
    return grad_input.reshape(image.shape), grad_in, grad_out, grad_kernel


def solution(mesh):
    placed = (
        P("scene", "tile", None, None, None),
        P(),
        P(),
        P(),
        P(),
        P(),
        P(),
        P(("scene", "tile"), None),
        P(("scene", "tile")),
        P(("scene", "tile"), None),
        P(("scene", "tile"), None),
    )
    return jax.shard_map(
        on_device,
        mesh=mesh,
        in_specs=placed,
        out_specs=(
            P("scene", "tile", None, None, None),
            P(("scene", "tile"), None),
            P(("scene", "tile"), None),
            P(),
        ),
        check_vma=False,
    )
```
